256 devices in a mesh: side: 2 (over x_lo), grp: 8 (over y, x_hi), shard: 16 (over z, core).
Axes of the slice: x: 4 (x_hi: 2, x_lo: 2; x = x_hi * 2 + x_lo), y: 4, z: 8, core: 2. Of those that a mesh axis runs over, the one named last changes fastest.
Arguments:
- queries: bfloat16 [512, 8192], P(('side', 'grp', 'shard')), may hold values from -80 to 80
- key_cache: bfloat16 [512, 192, 1024], P(('side', 'grp', 'shard')), may hold values from -4 to 4
- value_cache: bfloat16 [512, 192, 1024], P(('side', 'grp', 'shard')), may hold values from -8 to 8
- new_keys: bfloat16 [512, 1024], P(('side', 'grp', 'shard')), may hold values from -4 to 4
- new_values: bfloat16 [512, 1024], P(('side', 'grp', 'shard')), may hold values from -8 to 8
- lengths: int32 [512], P(('side', 'grp', 'shard')), may hold values from 1 to 192, as said below
- resid_in: bfloat16 [512, 8192], P(('side', 'grp', 'shard')), may hold values from -34 to 34
- norm_gain: bfloat16 [8192], replicated, may hold values from 0.099609375 to 1.8984375
- gate_weight: bfloat16 [53248, 8192], P(('side', 'grp', 'shard')), may hold values from -0.0625 to 0.0625
- up_weight: bfloat16 [53248, 8192], P(('side', 'grp', 'shard')), may hold values from -0.0625 to 0.0625
- down_weight: bfloat16 [53248, 8192], P(('side', 'grp', 'shard')), may hold values from -0.02734375 to 0.02734375
Outputs:
- attended: bfloat16 [512, 8192], P(('side', 'grp', 'shard'))
- ffn_out: bfloat16 [512, 8192], P(('side', 'grp', 'shard'))
The draws below stay inside these ranges and needn't reach their ends.
Inputs may be any that keep to these rules, and one draw needn't show every extreme that they name: Request r's cache holds data in its first lengths[r] slots; some request has exactly 192.
All inputs are finite; a program needn't handle non-finite values.
Results may differ from the reference program's by a relative error of at most 0.013.
Values may be sent and summed in bfloat16 or wider, within the bound.
A program may use at most 128 MiB of HBM per device.

```python
import jax
import jax.numpy as jnp
from jax import lax

D = 8192
HD = 128
HEADS = 64
KVH = 8
FF = 53248
REQ_DEV = 2
CACHE = 192
REQS = 512


def draw_queries(key, part):
    own_key = jax.random.fold_in(key, 11)
    drawn = jax.random.truncated_normal(own_key, -4.0, 4.0, (REQS, D), jnp.float32)
    return drawn.astype(jnp.bfloat16)


def draw_key_cache(key, part):
    own_key = jax.random.fold_in(key, 12)
    drawn = jax.random.truncated_normal(own_key, -4.0, 4.0, (REQS, CACHE, KVH * HD), jnp.float32)
    return drawn.astype(jnp.bfloat16)


def draw_new_keys(key, part):
    own_key = jax.random.fold_in(key, 13)
    drawn = jax.random.truncated_normal(own_key, -4.0, 4.0, (REQS, KVH * HD), jnp.float32)
    return drawn.astype(jnp.bfloat16)


def draw_resid_in(key, part):
    own_key = jax.random.fold_in(key, 14)
    key_values, key_rows, key_cols = jax.random.split(own_key, 3)
    row_scale = jnp.exp(jax.random.uniform(key_rows, (REQS, 1), jnp.float32, jnp.log(0.3), jnp.log(3.0)))
    col_scale = 0.316 * jnp.exp(jax.random.uniform(key_cols, (1, D), jnp.float32, 0.0, jnp.log(10.0)))
    values = jax.random.truncated_normal(key_values, -2.5, 2.5, (REQS, D), jnp.float32)
    return (values * row_scale * col_scale).astype(jnp.bfloat16)


def draw_lengths(key, part):
    own_key = jax.random.fold_in(key, 15)
    key_caps, key_lens, key_long = jax.random.split(own_key, 3)
    device_count = REQS // REQ_DEV
    caps = jax.random.randint(key_caps, (device_count,), CACHE // 4, CACHE + 1)
    cap_rows = jnp.repeat(caps, REQ_DEV, total_repeat_length=REQS)
    drawn = jax.random.randint(key_lens, (REQS,), 0, 1 << 20) % cap_rows + 1
    longest = jax.random.randint(key_long, (), 0, REQS)
    return jnp.where(jnp.arange(REQS) == longest, CACHE, drawn).astype(jnp.int32)


def steps_of(key, shape, shards, smallest, largest):
    def one(dim, blocks):
        steps = jax.random.uniform(jax.random.fold_in(jax.random.fold_in(key, 6), dim), (blocks,), jnp.float32, smallest / len(shards), largest / len(shards))
        return jnp.repeat(jnp.exp(steps), shape[dim] // blocks).reshape((-1,) + (1,) * (len(shape) - dim - 1))

    level = one(*shards[0])
    for cut in shards[1:]:
        level = level * one(*cut)
    return level


def bell_draw(rng, shape, width, reach, cuts=(), kind=jnp.bfloat16):
    factor_of = steps_of(rng, shape, cuts, -0.22, 0.18) if cuts else 1.0
    array = jax.random.normal(rng, shape, jnp.float32) * width * factor_of
    return jnp.minimum(jnp.maximum(array, -reach), reach).astype(kind)


def setup_inputs(seed: int = 0) -> dict:
    streams_of = jax.random.split(jax.random.key(seed), 12)
    queries = draw_queries(jax.random.fold_in(streams_of[11], 71), 0)
    key_cache = draw_key_cache(jax.random.fold_in(streams_of[11], 71), 0)
    value_cache = bell_draw(streams_of[2], (REQS, CACHE, KVH * HD), 2.0, 8.0, ((0, 256),))
    new_keys = draw_new_keys(jax.random.fold_in(streams_of[11], 71), 0)
    new_values = bell_draw(streams_of[4], (REQS, KVH * HD), 2.0, 8.0, ((0, 256),))
    lengths = draw_lengths(jax.random.fold_in(streams_of[11], 71), 0)
    resid_in = draw_resid_in(jax.random.fold_in(streams_of[11], 71), 0)
    norm_gain = jnp.clip(1.0 + 0.18 * jax.random.normal(streams_of[7], (D,), jnp.float32), 0.099609375, 1.8984375).astype(jnp.bfloat16)
    gate_weight = bell_draw(streams_of[8], (FF, D), D ** -0.5, 0.0625, ((0, 256),))
    up_weight = bell_draw(streams_of[9], (FF, D), D ** -0.5, 0.0625, ((0, 256),))
    down_weight = bell_draw(streams_of[10], (FF, D), FF ** -0.5, 0.02734375, ((0, 256),))
    return {"queries": queries, "key_cache": key_cache, "value_cache": value_cache, "new_keys": new_keys, "new_values": new_values, "lengths": lengths, "resid_in": resid_in, "norm_gain": norm_gain, "gate_weight": gate_weight, "up_weight": up_weight, "down_weight": down_weight}


NEG_FILL = -1e+30
EPSILON = 1e-05

def attend_one(query, cache_keys, cache_values, own_key, own_value, length):
    group_size = HEADS // KVH
    score_scale = HD ** (-0.5)
    query_heads = query.astype(jnp.float32).reshape(KVH, group_size, HD)
    keys_f = cache_keys.astype(jnp.float32).reshape(CACHE, KVH, HD)
    values_f = cache_values.astype(jnp.float32).reshape(CACHE, KVH, HD)
    scores = jnp.einsum('kgh,tkh->kgt', query_heads, keys_f) * score_scale
    is_valid = (jnp.arange(CACHE, dtype=jnp.int32) < length)[None, None, :]
    scores = jnp.where(is_valid, scores, NEG_FILL)
    own_score = jnp.einsum('kgh,kh->kg', query_heads, own_key.astype(jnp.float32).reshape(KVH, HD)) * score_scale
    top_score = jnp.maximum(lax.optimization_barrier(jnp.max(scores, axis=-1)), own_score)
    cache_exp = jnp.where(is_valid, jnp.exp(scores - top_score[..., None]), 0.0)
    own_exp = jnp.exp(own_score - top_score)
    total_sum = lax.optimization_barrier(jnp.sum(cache_exp, axis=-1)) + own_exp
    cache_probs = (cache_exp / total_sum[..., None]).astype(jnp.bfloat16)
    own_prob = (own_exp / total_sum).astype(jnp.bfloat16)
    mixed_heads = jnp.einsum('kgt,tkh->kgh', cache_probs.astype(jnp.float32), values_f)
    mixed_heads = mixed_heads + own_prob.astype(jnp.float32)[..., None] * own_value.astype(jnp.float32).reshape(KVH, 1, HD)
    return mixed_heads.reshape(KVH * group_size * HD)

def reference(queries, key_cache, value_cache, new_keys, new_values, lengths, resid_in, norm_gain, gate_weight, up_weight, down_weight):
    mixed_heads = lax.map(lambda packed: attend_one(*packed), (queries, key_cache, value_cache, new_keys, new_values, lengths))
    attended = (resid_in.astype(jnp.float32) + mixed_heads).astype(jnp.bfloat16)
    attended_f = lax.optimization_barrier(attended).astype(jnp.float32)
    mean_square = lax.optimization_barrier(jnp.mean(attended_f * attended_f, axis=1, keepdims=True))
    normed = (attended_f * lax.rsqrt(mean_square + EPSILON) * norm_gain.astype(jnp.float32)).astype(jnp.bfloat16)
    normed_f = normed.astype(jnp.float32)
    gate_proj = jnp.dot(normed_f, gate_weight.astype(jnp.float32).T, preferred_element_type=jnp.float32)
    upward = jnp.dot(normed_f, up_weight.astype(jnp.float32).T, preferred_element_type=jnp.float32)
    hidden = (jax.nn.silu(gate_proj) * upward).astype(jnp.bfloat16)
    ffn_out = jnp.dot(hidden.astype(jnp.float32), down_weight.astype(jnp.float32), preferred_element_type=jnp.float32).astype(jnp.bfloat16)
    return (attended, ffn_out)
```

```python
import jax
import jax.numpy as jnp
from jax import lax
from jax.experimental import pallas as pl
from jax.experimental.pallas import tpu as pltpu
from jax.sharding import PartitionSpec as P

MESH = pl.DeviceIdType.MESH
F32 = jnp.float32
BF16 = jnp.bfloat16

HD = 128
KVH = 8
CACHE = 192
UNITS = 208
EPSILON = 1e-05
NEG_FILL = -1e30

RING4 = (0, 1, -1, 2)
BACK4 = (0, 2, 1, 3)
GROUPS = ((0, 1), (1, 3), (3, 5), (5, 7), (7, 8))
PLANE = 4096
PART = 2048
HALF = 1024
HALVES = (pl.ds(0, HALF), pl.ds(HALF, HALF))


def kernel(
    q_ref, resid_ref, newk_ref, newv_ref, len_ref, gain_ref,
    k_hbm, v_hbm, gate_hbm, up_hbm, down_hbm,
    att_ref, ffn_ref,
    kb, vb, wg, wu, wd, qs, rs_, at, ns, r1, xs, pa, pn, pr, haf, hab, hbb,
    tb, un, fr, cr, zs, zr, qf, ff,
    send_sems, recv_sems, local_sems,
):
    side = lax.axis_index("side")
    grp = lax.axis_index("grp")
    shard = lax.axis_index("shard")
    x = lax.rem(grp, 2) * 2 + side
    y = grp // 2
    z = shard // 2
    c = lax.rem(shard, 2)
    oc = 1 - c

    def device(dx=0, dy=0, dz=0, core=c):
        xx = lax.rem(x + dx + 4, 4)
        yy = lax.rem(y + dy + 4, 4)
        zz = lax.rem(z + dz + 8, 8)
        return (lax.rem(xx, 2), yy * 2 + xx // 2, zz * 2 + core)

    def along(part, d, core=c):
        return device(dx=d, core=core) if part == 0 else device(dy=d, core=core)

    def across(part, d, core=c):
        return along(1 - part, d, core)

    sends = []
    counts = [0, 0]

    def remote(src, dst, target):
        i = counts[0]
        counts[0] += 1
        copy = pltpu.make_async_remote_copy(
            src_ref=src, dst_ref=dst, send_sem=send_sems.at[i], recv_sem=recv_sems.at[i],
            device_id=target, device_id_type=MESH,
        )
        copy.start()
        sends.append(copy)
        return copy

    def local(src, dst):
        i = counts[1]
        counts[1] += 1
        copy = pltpu.make_async_copy(src, dst, local_sems.at[i])
        copy.start()
        return copy

    barrier = pltpu.get_barrier_semaphore()
    peers = [device(core=oc), device(dz=1), device(dz=-1)]
    for d in RING4[1:]:
        for core in (c, oc):
            peers.append(device(dx=d, core=core))
            peers.append(device(dy=d, core=core))
    for peer in peers:
        pl.semaphore_signal(barrier, inc=1, device_id=peer, device_id_type=MESH)

    cache_loads = [local(k_hbm, kb), local(v_hbm, vb)]
    mine = pl.ds(pl.multiple_of(c * UNITS, 16), UNITS)
    own_cols = pl.ds(pl.multiple_of(c * PLANE, PLANE), PLANE)
    other_cols = pl.ds(pl.multiple_of(oc * PLANE, PLANE), PLANE)
    weights = ((gate_hbm, wg), (up_hbm, wu), (down_hbm, wd))
    weight_loads = [local(h.at[:, own_cols], w.at[mine]) for h, w in weights]

    pl.semaphore_wait(barrier, len(peers))
    weight_swaps = [remote(h.at[:, other_cols], w.at[mine], device(core=oc)) for h, w in weights]

    qv = q_ref[...].astype(F32)
    rv = resid_ref[...].astype(F32)
    for j in range(64):
        qs[pl.ds(j, 2, stride=64), :] = qv[:, j * HD:(j + 1) * HD]
        rs_[pl.ds(j, 2, stride=64), :] = rv[:, j * HD:(j + 1) * HD]
    newk = newk_ref[...].astype(F32)
    newv = newv_ref[...].astype(F32)
    row = lax.broadcasted_iota(jnp.int32, (16, 2 * CACHE), 0)
    col = lax.broadcasted_iota(jnp.int32, (16, 2 * CACHE), 1)
    slot_of = jnp.where(row < 8, col, col - CACHE)
    filled = jnp.where(row < 8, len_ref[0], len_ref[1])
    valid = (slot_of >= 0) & (slot_of < filled)
    for load in cache_loads:
        load.wait()
    first = lax.broadcasted_iota(jnp.int32, (16, HD), 0) < 8

    def both(rows, k):
        one = rows[0:1, k * HD:(k + 1) * HD]
        two = rows[1:2, k * HD:(k + 1) * HD]
        return jnp.where(first, one, two)

    scale = HD ** (-0.5)
    scored = []
    for k in range(KVH):
        q16 = jnp.concatenate([qs[8 * k:8 * k + 8, :], qs[64 + 8 * k:72 + 8 * k, :]], axis=0)
        keys = kb[:, :, k * HD:(k + 1) * HD].reshape(2 * CACHE, HD)
        s = lax.dot_general(
            q16.astype(BF16), keys, (((1,), (1,)), ((), ())), preferred_element_type=F32
        ) * scale
        own = jnp.sum(q16 * both(newk, k), axis=1, keepdims=True) * scale
        scored.append((jnp.where(valid, s, NEG_FILL), own))
    weighted = []
    for s, own in scored:
        top = jnp.maximum(jnp.max(s, axis=1, keepdims=True), own)
        e = jnp.where(valid, jnp.exp(s - top), 0.0)
        own_e = jnp.exp(own - top)
        total = jnp.sum(e, axis=1, keepdims=True) + own_e
        weighted.append(((e / total).astype(BF16), (own_e / total).astype(BF16).astype(F32)))
    for k, (p, own_p) in enumerate(weighted):
        values = vb[:, :, k * HD:(k + 1) * HD].reshape(2 * CACHE, HD)
        mixed = jnp.dot(p, values, preferred_element_type=F32) + own_p * both(newv, k)
        for r in range(2):
            rows = pl.ds(r * 64 + 8 * k, 8)
            at[rows, :] = (rs_[rows, :] + mixed[8 * r:8 * r + 8]).astype(BF16).astype(F32)

    gain = gain_ref[...].astype(F32)
    for r in range(2):
        a = at[r * 64:(r + 1) * 64, :]
        mean_square = jnp.sum(a * a, keepdims=True).reshape(1, 1) * (1.0 / 8192)
        normed = (a * lax.rsqrt(mean_square + EPSILON) * gain).astype(BF16).astype(F32)
        for plane in range(2):
            for part in range(2):
                j = plane * 32 + part * 16
                ns[part, plane, r * 16:(r + 1) * 16, :] = normed[j:j + 16]

    def src_rows(slot, core):
        return pl.ds(pl.multiple_of((slot * 2 + core) * 32, 32), 32)

    first_copies = []
    for part in range(2):
        for d in (2, 1, -1):
            slot = BACK4[RING4.index(d)]
            for core in (c, oc):
                first_copies.append((part, remote(
                    ns.at[part, core], r1.at[part, src_rows(slot, c)], across(part, d, core))))
        first_copies.append((part, remote(
            ns.at[part, oc], r1.at[part, src_rows(0, c)], device(core=oc))))
        r1[part, src_rows(0, c), :] = ns[part, c]
    for j in range(64):
        att_ref[:, j * HD:(j + 1) * HD] = at[pl.ds(j, 2, stride=64), :].astype(BF16)

    z_copies = {}
    x_copies = {}
    f_copies = {}

    def z_send(part, k):
        ahead, behind = 2 * k, max(2 * k - 1, 0)
        if k < 3:
            z_copies[part, k] = (
                remote(xs.at[part, ahead, 0], xs.at[part, 2 * k + 2, 0], device(dz=1)),
                remote(xs.at[part, behind, 0], xs.at[part, 2 * k + 1, 0], device(dz=-1)),
            )
        else:
            z_copies[part, k] = tuple(
                remote(xs.at[part, s, 0, :, h], xs.at[part, 7, 0, :, h], device(dz=d))
                for s, h, d in ((ahead, HALVES[0], 1), (behind, HALVES[1], -1))
            )

    def x_send(part, g):
        zz = pl.ds(GROUPS[g][0], GROUPS[g][1] - GROUPS[g][0])
        x_copies[part, g] = (
            remote(xs.at[part, zz, 0], xs.at[part, zz, 2], along(part, 1)),
            remote(xs.at[part, zz, 0], xs.at[part, zz, 1], along(part, -1)),
        )

    def x_forward(part, g):
        zz = pl.ds(GROUPS[g][0], GROUPS[g][1] - GROUPS[g][0])
        x_copies[part, g][0].wait_recv()
        far0 = remote(xs.at[part, zz, 2, :, HALVES[0]], xs.at[part, zz, 3, :, HALVES[0]], along(part, 1))
        x_copies[part, g][1].wait_recv()
        far1 = remote(xs.at[part, zz, 1, :, HALVES[1]], xs.at[part, zz, 3, :, HALVES[1]], along(part, -1))
        f_copies[part, g] = (far0, far1)

    for part in range(2):
        for p, copy in first_copies:
            if p == part:
                copy.wait_recv()
        for j in range(16):
            xs[part, 0, 0, :, j * HD:(j + 1) * HD] = r1[part, pl.ds(j, 16, stride=16), :].astype(BF16)
        z_send(part, 0)
        x_send(part, 0)

    p_copies = {}
    far_copies = {}
    near_copies = {}

    def gates(g):
        a, b = GROUPS[g]
        n, m = b - a, 64 * (b - a)
        rows = pl.ds(a * 64, m)
        for part in range(2):
            for copy in f_copies[part, g]:
                copy.wait_recv()
        for i, w in enumerate((wg, wu)):
            dots = [
                lax.dot_general(
                    xs[part, a:b].reshape(m, PART), w[:, part * PART:(part + 1) * PART],
                    (((1,), (1,)), ((), ())), preferred_element_type=F32,
                ) for part in range(2)
            ]
            for s in range(n):
                for u in range(4):
                    for v in range(4):
                        pa[i, s * 64 + u * 16 + v * 4:s * 64 + u * 16 + v * 4 + 4, :] = (
                            dots[0][s * 64 + v * 16 + u * 4:s * 64 + v * 16 + u * 4 + 4])
            pn[i, rows, :] = pa[i, :m, :] + dots[1]
        p_copies[g] = remote(pn.at[:, rows], pr.at[:, rows], device(core=oc))

    def hidden_down(g):
        a, b = GROUPS[g]
        n, m = b - a, 64 * (b - a)
        rows = pl.ds(a * 64, m)
        p_copies[g].wait_recv()
        gate = pn[0, rows, :] + pr[0, rows, :]
        up = pn[1, rows, :] + pr[1, rows, :]
        hidden = gate / (1.0 + jnp.exp(-gate)) * up
        hbb[:m, :] = hidden.astype(BF16)
        for s in range(n):
            for u in range(4):
                for v in range(4):
                    haf[s * 64 + u * 16 + v * 4:s * 64 + u * 16 + v * 4 + 4, :] = (
                        hidden[s * 64 + v * 16 + u * 4:s * 64 + v * 16 + u * 4 + 4])
        hab[:m, :] = haf[:m, :].astype(BF16)
        zz = pl.ds(a, n)
        for part, h in enumerate((hab, hbb)):
            for t in range(4):
                cols = pl.ds(t * 512, 512)
                term = jnp.dot(
                    h[:m, :], wd[:, part * PART + t * 512:part * PART + (t + 1) * 512],
                    preferred_element_type=F32,
                ).reshape(n, 4, 16, 512)
                un[part, zz, :, cols] = term[:, 0]
                tb[part, zz, :, :, cols] = term[:, 1:].astype(BF16)
            far_copies[part, g] = tuple(
                remote(tb.at[part, zz, 2, :, HALVES[i]], fr.at[part, i, zz], along(part, d))
                for i, d in enumerate((1, -1))
            )

    def relay(g):
        zz = pl.ds(GROUPS[g][0], GROUPS[g][1] - GROUPS[g][0])
        for part in range(2):
            copies = []
            for i, d in enumerate((1, -1)):
                far_copies[part, g][i].wait_recv()
                near = tb[part, zz, i, :, HALVES[i]].astype(F32) + fr[part, i, zz].astype(F32)
                tb[part, zz, i, :, HALVES[i]] = near.astype(BF16)
                copies.append(remote(tb.at[part, zz, i], cr.at[part, i, zz], along(part, d)))
            near_copies[part, g] = copies

    def collect(g):
        zz = pl.ds(GROUPS[g][0], GROUPS[g][1] - GROUPS[g][0])
        for part in range(2):
            for copy in near_copies[part, g]:
                copy.wait_recv()
            un[part, zz] = un[part, zz] + (cr[part, 0, zz].astype(F32) + cr[part, 1, zz].astype(F32))

    def z_step(k):
        for part in range(2):
            for copy in z_copies[part, k - 1]:
                copy.wait_recv()
            if k < 4:
                z_send(part, k)
            x_send(part, k)

    def forward(g):
        for part in range(2):
            x_forward(part, g)

    z_step(1)
    forward(0)
    z_step(2)
    forward(1)
    for copy in weight_loads:
        copy.wait()
    for copy in weight_swaps:
        copy.wait_recv()
    gates(0)
    z_step(3)
    forward(2)
    gates(1)
    hidden_down(0)
    z_step(4)
    forward(3)
    gates(2)
    hidden_down(1)
    relay(0)
    forward(4)
    gates(3)
    hidden_down(2)
    relay(1)
    collect(0)
    gates(4)
    hidden_down(3)
    relay(2)
    collect(1)
    hidden_down(4)
    relay(3)
    collect(2)
    relay(4)
    collect(3)
    collect(4)

    zc = {}
    for step in range(5):
        for part in range(2):
            if step > 0:
                for copy in zc[part, step - 1]:
                    copy.wait_recv()
            if step == 4:
                un[part, 0] = un[part, 0] + (zr[part, 0, 3].astype(F32) + zr[part, 1, 3].astype(F32))
                continue
            copies = []
            for i, d in enumerate((1, -1)):
                if step == 0:
                    zs[part, i, 0, :, HALVES[i]] = un[part, 7, :, HALVES[i]].astype(BF16)
                    copies.append(remote(
                        zs.at[part, i, 0, :, HALVES[i]], zr.at[part, i, 0, :, HALVES[i]], device(dz=d)))
                    continue
                block = 2 * (4 - step) - 1 + i
                if step == 1:
                    zs[part, i, 1, :, HALVES[1 - i]] = un[part, block, :, HALVES[1 - i]].astype(BF16)
                    zs[part, i, 1, :, HALVES[i]] = (
                        un[part, block, :, HALVES[i]] + zr[part, i, 0, :, HALVES[i]].astype(F32)).astype(BF16)
                else:
                    zs[part, i, step] = (un[part, block] + zr[part, i, step - 1].astype(F32)).astype(BF16)
                copies.append(remote(zs.at[part, i, step], zr.at[part, i, step], device(dz=d)))
            zc[part, step] = copies

    last_copies = []
    for part in range(2):
        for j in range(16):
            qf[part, pl.ds(j, 16, stride=16), :] = un[part, 0, :, j * HD:(j + 1) * HD]
        for s, d in ((3, 2), (1, 1), (2, -1)):
            for core in (c, oc):
                last_copies.append(remote(
                    qf.at[part, src_rows(s, core)], ff.at[part, c, BACK4[s]], across(part, d, core)))
        last_copies.append(remote(qf.at[part, src_rows(0, oc)], ff.at[part, c, 0], device(core=oc)))
        ff[part, c, 0] = qf[part, src_rows(0, c), :]
    for copy in last_copies:
        copy.wait_recv()
    for plane in range(2):
        for part in range(2):
            total = (ff[part, plane, 0] + ff[part, plane, 1]) + (ff[part, plane, 2] + ff[part, plane, 3])
            qs[0:32, :] = total
            for j in range(16):
                first_col = (plane * 32 + part * 16 + j) * HD
                ffn_ref[:, first_col:first_col + HD] = qs[pl.ds(j, 2, stride=16), :].astype(BF16)
    for copy in sends:
        copy.wait_send()


N_REMOTE = 3 + 14 + 16 + 20 + 20 + 5 + 20 + 20 + 16 + 14


def local(
    queries, key_cache, value_cache, new_keys, new_values, lengths, resid_in, norm_gain,
    gate_weight, up_weight, down_weight,
):
    vmem = pl.BlockSpec(memory_space=pltpu.VMEM)
    smem = pl.BlockSpec(memory_space=pltpu.SMEM)
    hbm = pl.BlockSpec(memory_space=pl.ANY)
    out = jax.ShapeDtypeStruct((2, 8192), BF16)
    return pl.pallas_call(
        kernel,
        out_shape=(out, out),
        in_specs=[vmem, vmem, vmem, vmem, smem, vmem] + [hbm] * 5,
        out_specs=(vmem, vmem),
        scratch_shapes=[
            pltpu.VMEM((2, CACHE, 1024), BF16),
            pltpu.VMEM((2, CACHE, 1024), BF16),
            pltpu.VMEM((2 * UNITS, PLANE), BF16),
            pltpu.VMEM((2 * UNITS, PLANE), BF16),
            pltpu.VMEM((2 * UNITS, PLANE), BF16),
            pltpu.VMEM((128, 128), F32),
            pltpu.VMEM((128, 128), F32),
            pltpu.VMEM((128, 128), F32),
            pltpu.VMEM((2, 2, 32, 128), F32),
            pltpu.VMEM((2, 256, 128), F32),
            pltpu.VMEM((2, 8, 4, 16, PART), BF16),
            pltpu.VMEM((2, 128, 2 * UNITS), F32),
            pltpu.VMEM((2, 512, 2 * UNITS), F32),
            pltpu.VMEM((2, 512, 2 * UNITS), F32),
            pltpu.VMEM((128, 2 * UNITS), F32),
            pltpu.VMEM((128, 2 * UNITS), BF16),
            pltpu.VMEM((128, 2 * UNITS), BF16),
            pltpu.VMEM((2, 8, 3, 16, PART), BF16),
            pltpu.VMEM((2, 8, 16, PART), F32),
            pltpu.VMEM((2, 2, 8, 16, HALF), BF16),
            pltpu.VMEM((2, 2, 8, 16, PART), BF16),
            pltpu.VMEM((2, 2, 4, 16, PART), BF16),
            pltpu.VMEM((2, 2, 4, 16, PART), BF16),
            pltpu.VMEM((2, 256, 128), F32),
            pltpu.VMEM((2, 2, 4, 32, 128), F32),
            pltpu.SemaphoreType.DMA((N_REMOTE,)),
            pltpu.SemaphoreType.DMA((N_REMOTE,)),
            pltpu.SemaphoreType.DMA((5,)),
        ],
        compiler_params=pltpu.CompilerParams(
            collective_id=0, has_side_effects=True, vmem_limit_bytes=56 * 2**20
        ),
        name="decode_layer",
    )(
        queries, resid_in, new_keys, new_values, lengths, norm_gain.reshape(64, 128),
        key_cache, value_cache, gate_weight, up_weight, down_weight,
    )


def solution(mesh):
    rows = P(("side", "grp", "shard"), None)
    cache = P(("side", "grp", "shard"), None, None)
    return jax.shard_map(
        local,
        mesh=mesh,
        in_specs=(rows, cache, cache, rows, rows, P(("side", "grp", "shard")), rows, P(), rows, rows, rows),
        out_specs=(rows, rows),
        check_vma=False,
    )
```

```python
import jax
import jax.numpy as jnp
from jax import lax
from jax.experimental import pallas as pl
from jax.experimental.pallas import tpu as pltpu
from jax.sharding import PartitionSpec as P

MESH = pl.DeviceIdType.MESH
F32 = jnp.float32
BF16 = jnp.bfloat16

HD = 128
KVH = 8
CACHE = 192
UNITS = 208
EPSILON = 1e-05
NEG_FILL = -1e30

RING4 = (0, 1, -1, 2)
BACK4 = (0, 2, 1, 3)
GROUPS = ((0, 1), (1, 3), (3, 5), (5, 7), (7, 8))
DOTS = ((0, 1), (2,), (3, 4))
RUNS = ((0, 3), (3, 5), (5, 8))
BACKS = ((0, 3), (3, 5), (7, 8), (5, 7))
PLANE = 4096
PART = 2048
HALF = 1024
HALVES = (pl.ds(0, HALF), pl.ds(HALF, HALF))


def kernel(
    q_ref, resid_ref, newk_ref, newv_ref, len_ref, gain_ref,
    k_hbm, v_hbm, gate_hbm, up_hbm, down_hbm,
    out_ref,
    kb, vb, wg, wu, wd, qs, rs_, at, ns, r1, ex, xs, pa, pn, pr, haf, hab, hbb,
    tb, un, fr, cr, zs, zr, qf, ff,
    send_sems, recv_sems, local_sems,
):
    side = lax.axis_index("side")
    grp = lax.axis_index("grp")
    shard = lax.axis_index("shard")
    x = lax.rem(grp, 2) * 2 + side
    y = grp // 2
    z = shard // 2
    c = lax.rem(shard, 2)
    oc = 1 - c

    def device(dx=0, dy=0, dz=0, core=c):
        xx = lax.rem(x + dx + 4, 4)
        yy = lax.rem(y + dy + 4, 4)
        zz = lax.rem(z + dz + 8, 8)
        return (lax.rem(xx, 2), yy * 2 + xx // 2, zz * 2 + core)

    def along(part, d, core=c):
        return device(dx=d, core=core) if part == 0 else device(dy=d, core=core)

    def across(part, d, core=c):
        return along(1 - part, d, core)

    send_ids = {}
    recv_ids = {}

    def remote(src, dst, target, sent, got):
        i = send_ids.setdefault(sent, len(send_ids))
        j = recv_ids.setdefault(got, len(recv_ids))
        pltpu.make_async_remote_copy(
            src_ref=src, dst_ref=dst, send_sem=send_sems.at[i], recv_sem=recv_sems.at[j],
            device_id=target, device_id_type=MESH,
        ).start()

    def wait_sent(sent, ref):
        pltpu.make_async_copy(ref, ref, send_sems.at[send_ids[sent]]).wait()

    def wait_got(got, ref):
        pltpu.make_async_copy(ref, ref, recv_sems.at[recv_ids[got]]).wait()

    loads = []

    def local(src, dst):
        i = len(loads)
        loads.append(i)
        copy = pltpu.make_async_copy(src, dst, local_sems.at[i])
        copy.start()
        return copy

    barrier = pltpu.get_barrier_semaphore()
    peers = [device(core=oc), device(dz=1), device(dz=-1)]
    for d in RING4[1:]:
        for core in (c, oc):
            peers.append(device(dx=d, core=core))
            peers.append(device(dy=d, core=core))
    for peer in peers:
        pl.semaphore_signal(barrier, inc=1, device_id=peer, device_id_type=MESH)

    cache_loads = [local(k_hbm, kb), local(v_hbm, vb)]
    mine = pl.ds(pl.multiple_of(c * UNITS, 16), UNITS)
    own_cols = pl.ds(pl.multiple_of(c * PLANE, PLANE), PLANE)
    other_cols = pl.ds(pl.multiple_of(oc * PLANE, PLANE), PLANE)
    weights = ((gate_hbm, wg), (up_hbm, wu), (down_hbm, wd))
    weight_loads = [local(h.at[:, own_cols], w.at[mine]) for h, w in weights]

    qv = q_ref[...].astype(F32)
    rv = resid_ref[...].astype(F32)
    for j in range(64):
        qs[pl.ds(j, 2, stride=64), :] = qv[:, j * HD:(j + 1) * HD]
        rs_[pl.ds(j, 2, stride=64), :] = rv[:, j * HD:(j + 1) * HD]
    newk = newk_ref[...].astype(F32)
    newv = newv_ref[...].astype(F32)
    row = lax.broadcasted_iota(jnp.int32, (16, 2 * CACHE), 0)
    col = lax.broadcasted_iota(jnp.int32, (16, 2 * CACHE), 1)
    slot_of = jnp.where(row < 8, col, col - CACHE)
    filled = jnp.where(row < 8, len_ref[0], len_ref[1])
    valid = (slot_of >= 0) & (slot_of < filled)
    for load in cache_loads:
        load.wait()
    first = lax.broadcasted_iota(jnp.int32, (16, HD), 0) < 8

    def both(rows, k):
        one = rows[0:1, k * HD:(k + 1) * HD]
        two = rows[1:2, k * HD:(k + 1) * HD]
        return jnp.where(first, one, two)

    scale = HD ** (-0.5)
    scored = []
    for k in range(KVH):
        q16 = jnp.concatenate([qs[8 * k:8 * k + 8, :], qs[64 + 8 * k:72 + 8 * k, :]], axis=0)
        keys = kb[:, :, k * HD:(k + 1) * HD].reshape(2 * CACHE, HD)
        s = lax.dot_general(
            q16.astype(BF16), keys, (((1,), (1,)), ((), ())), preferred_element_type=F32
        ) * scale
        own = jnp.sum(q16 * both(newk, k), axis=1, keepdims=True) * scale
        scored.append((jnp.where(valid, s, NEG_FILL), own))
    weighted = []
    for s, own in scored:
        top = jnp.maximum(jnp.max(s, axis=1, keepdims=True), own)
        e = jnp.where(valid, jnp.exp(s - top), 0.0)
        own_e = jnp.exp(own - top)
        total = jnp.sum(e, axis=1, keepdims=True) + own_e
        weighted.append(((e / total).astype(BF16), (own_e / total).astype(BF16).astype(F32)))
    for k, (p, own_p) in enumerate(weighted):
        values = vb[:, :, k * HD:(k + 1) * HD].reshape(2 * CACHE, HD)
        mixed = jnp.dot(p, values, preferred_element_type=F32) + own_p * both(newv, k)
        for r in range(2):
            rows = pl.ds(r * 64 + 8 * k, 8)
            at[rows, :] = (rs_[rows, :] + mixed[8 * r:8 * r + 8]).astype(BF16).astype(F32)

    gain = gain_ref[...].astype(F32)
    for r in range(2):
        a = at[r * 64:(r + 1) * 64, :]
        mean_square = jnp.sum(a * a, keepdims=True).reshape(1, 1) * (1.0 / 8192)
        normed = (a * lax.rsqrt(mean_square + EPSILON) * gain).astype(BF16)
        for plane in range(2):
            for part in range(2):
                j = plane * 32 + part * 16
                ns[part, plane, r * 16:(r + 1) * 16, :] = normed[j:j + 16]

    pl.semaphore_wait(barrier, len(peers))

    def src_rows(slot, core):
        return pl.ds(pl.multiple_of((slot * 2 + core) * 32, 32), 32)

    for part in range(2):
        for d in (2, 1, -1):
            slot = BACK4[RING4.index(d)]
            for core in (c, oc):
                remote(ns.at[part, core], r1.at[part, src_rows(slot, c)], across(part, d, core), "first", ("first", part))
        remote(ns.at[part, oc], r1.at[part, src_rows(0, c)], device(core=oc), "first", ("first", part))
        r1[part, src_rows(0, c), :] = ns[part, c]
    for i, (h, w) in enumerate(weights):
        remote(h.at[:, other_cols], w.at[mine], device(core=oc), ("weight", i), ("weight", i))
    for j in range(64):
        out_ref[0:2, j * HD:(j + 1) * HD] = at[pl.ds(j, 2, stride=64), :].astype(BF16)

    def z_send(part, k):
        ahead, behind = 2 * k, max(2 * k - 1, 0)
        sent, got = "z", ("z", part, k)
        if k < 3:
            remote(xs.at[part, ahead, 0], xs.at[part, 2 * k + 2, 0], device(dz=1), sent, got)
            remote(xs.at[part, behind, 0], xs.at[part, 2 * k + 1, 0], device(dz=-1), sent, got)
        else:
            for s, h, d in ((ahead, HALVES[0], 1), (behind, HALVES[1], -1)):
                remote(xs.at[part, s, 0, :, h], xs.at[part, 7, 0, :, h], device(dz=d), sent, got)

    def z_wait(part, k):
        wait_got(("z", part, k), xs.at[part, 2 * k + 1:2 * k + 3, 0] if k < 3 else xs.at[part, 7, 0])

    def x_send(part, g):
        zz = pl.ds(GROUPS[g][0], GROUPS[g][1] - GROUPS[g][0])
        remote(xs.at[part, zz, 0], xs.at[part, zz, 2], along(part, 1), "x", ("x", part, g))
        remote(xs.at[part, zz, 0], xs.at[part, zz, 1], along(part, -1), "x", ("x", part, g))

    def x_forward(part, g):
        zz = pl.ds(GROUPS[g][0], GROUPS[g][1] - GROUPS[g][0])
        wait_got(("x", part, g), xs.at[part, zz, 1:3])
        for s, h, d in ((2, HALVES[0], 1), (1, HALVES[1], -1)):
            remote(xs.at[part, zz, s, :, h], xs.at[part, zz, 3, :, h], along(part, d), "x", ("far", part, g))

    for part in range(2):
        wait_got(("first", part), r1.at[part, 0:224])
        ex[...] = r1[part].astype(F32)
        for j in range(16):
            xs[part, 0, 0, :, j * HD:(j + 1) * HD] = ex[pl.ds(j, 16, stride=16), :].astype(BF16)
        z_send(part, 0)
        x_send(part, 0)

    def gates(g, i):
        a, b = RUNS[g]
        n, m = b - a, 64 * (b - a)
        rows = pl.ds(a * 64, m)
        if i == 0:
            for part in range(2):
                for one in DOTS[g]:
                    wait_got(("far", part, one), xs.at[part, GROUPS[one][0]:GROUPS[one][1], 3])
        dots = [
            lax.dot_general(
                xs[part, a:b].reshape(m, PART), (wg, wu)[i][:, part * PART:(part + 1) * PART],
                (((1,), (1,)), ((), ())), preferred_element_type=F32,
            ) for part in range(2)
        ]
        for s in range(n):
            for u in range(4):
                for v in range(4):
                    pa[i, s * 64 + u * 16 + v * 4:s * 64 + u * 16 + v * 4 + 4, :] = (
                        dots[0][s * 64 + v * 16 + u * 4:s * 64 + v * 16 + u * 4 + 4])
        pn[i, rows, :] = pa[i, :m, :] + dots[1]
        remote(pn.at[i, rows], pr.at[i, rows], device(core=oc), "dots", ("dots", i, g))

    def hidden_down(g):
        a, b = RUNS[g]
        n, m = b - a, 64 * (b - a)
        rows = pl.ds(a * 64, m)
        wait_got(("dots", 0, g), pr.at[0, rows])
        gate = pn[0, rows, :] + pr[0, rows, :]
        wait_got(("dots", 1, g), pr.at[1, rows])
        up = pn[1, rows, :] + pr[1, rows, :]
        hidden = gate / (1.0 + jnp.exp(-gate)) * up
        hbb[:m, :] = hidden.astype(BF16)
        for s in range(n):
            for u in range(4):
                for v in range(4):
                    haf[s * 64 + u * 16 + v * 4:s * 64 + u * 16 + v * 4 + 4, :] = (
                        hidden[s * 64 + v * 16 + u * 4:s * 64 + v * 16 + u * 4 + 4])
        hab[:m, :] = haf[:m, :].astype(BF16)
        zz = pl.ds(a, n)
        for part, h in enumerate((hab, hbb)):
            for t in range(4):
                cols = pl.ds(t * 512, 512)
                term = jnp.dot(
                    h[:m, :], wd[:, part * PART + t * 512:part * PART + (t + 1) * 512],
                    preferred_element_type=F32,
                ).reshape(n, 4, 16, 512)
                un[part, zz, :, cols] = term[:, 0]
                tb[part, zz, :, :, cols] = term[:, 1:].astype(BF16)

    def depart(g):
        zz = pl.ds(BACKS[g][0], BACKS[g][1] - BACKS[g][0])
        for part in range(2):
            for i, d in enumerate((1, -1)):
                remote(tb.at[part, zz, 2, :, HALVES[i]], fr.at[part, i, zz], along(part, d), "sum", ("relay", part, g))
        for part in range(2):
            for i, d in enumerate((1, -1)):
                h = HALVES[1 - i]
                remote(tb.at[part, zz, i, :, h], cr.at[part, i, zz, :, h], along(part, d), "sum", ("near", part, g))

    def relay(g):
        zz = pl.ds(BACKS[g][0], BACKS[g][1] - BACKS[g][0])
        for part in range(2):
            wait_got(("relay", part, g), fr.at[part, :, zz])
            for i, d in enumerate((1, -1)):
                h = HALVES[i]
                near = tb[part, zz, i, :, h].astype(F32) + fr[part, i, zz].astype(F32)
                tb[part, zz, i, :, h] = near.astype(BF16)
                remote(tb.at[part, zz, i, :, h], cr.at[part, i, zz, :, h], along(part, d), "sum", ("near", part, g))

    def collect(g):
        zz = pl.ds(BACKS[g][0], BACKS[g][1] - BACKS[g][0])
        for part in range(2):
            wait_got(("near", part, g), cr.at[part, :, zz])
            un[part, zz] = un[part, zz] + (cr[part, 0, zz].astype(F32) + cr[part, 1, zz].astype(F32))

    def z_step(k):
        for part in range(2):
            z_wait(part, k - 1)
            if k < 4:
                z_send(part, k)
            x_send(part, k)

    def forward(g):
        for part in range(2):
            x_forward(part, g)

    def z_sum(step):
        for h in range(2):
            for part in range(2):
                hh = HALVES[h]
                if step > 0:
                    got = ("zsum", part, h, step - 1)
                    wait_got(got, zr.at[part, 0, 0, :, hh] if step == 1 else zr.at[part, :, step - 1, :, hh])
                if step == 4:
                    un[part, 0, :, hh] = un[part, 0, :, hh] + (
                        zr[part, 0, 3, :, hh].astype(F32) + zr[part, 1, 3, :, hh].astype(F32))
                    continue
                for i, d in enumerate((1, -1)):
                    if step == 0 and i != h:
                        continue
                    total = un[part, 7 if step == 0 else 2 * (4 - step) - 1 + i, :, hh]
                    if step > 1 or (step == 1 and i == h):
                        total = total + zr[part, i, step - 1, :, hh].astype(F32)
                    zs[part, i, step, :, hh] = total.astype(BF16)
                    remote(zs.at[part, i, step, :, hh], zr.at[part, i, step, :, hh], device(dz=d),
                           "zsum", ("zsum", part, h, step))

    z_step(1)
    forward(0)
    z_step(2)
    forward(1)
    z_step(3)
    forward(2)
    for copy in weight_loads:
        copy.wait()
    for i, (h, w) in enumerate(weights):
        wait_got(("weight", i), w.at[mine])
    gates(0, 0)
    z_step(4)
    gates(0, 1)
    forward(3)
    gates(1, 0)
    forward(4)
    gates(1, 1)
    hidden_down(0)
    depart(0)
    gates(2, 0)
    gates(2, 1)
    hidden_down(1)
    relay(0)
    hidden_down(2)
    depart(2)
    depart(3)
    collect(0)
    relay(2)
    relay(3)
    depart(1)
    collect(2)
    z_sum(0)
    collect(3)
    z_sum(1)
    relay(1)
    collect(1)
    z_sum(2)
    z_sum(3)
    z_sum(4)

    for part in range(2):
        for j in range(16):
            ex[pl.ds(j, 16, stride=16), :] = un[part, 0, :, j * HD:(j + 1) * HD]
        qf[part] = ex[...].astype(BF16)
        for s, d in ((3, 2), (1, 1), (2, -1)):
            for core in (c, oc):
                remote(qf.at[part, src_rows(s, core)], ff.at[part, c, BACK4[s]], across(part, d, core), "last", "last")
        remote(qf.at[part, src_rows(0, oc)], ff.at[part, c, 0], device(core=oc), "last", "last")
        ff[part, c, 0] = qf[part, src_rows(0, c), :]
    for sent, ref in (
        ("first", r1.at[:, 0:224]), ("z", xs.at[:, 0:7, 0]), ("x", xs.at[:, :, 0:3]), ("dots", pn),
        ("sum", tb), ("zsum", xs.at[:, 0:7, 0]),
    ):
        wait_sent(sent, ref)
    for i, (h, w) in enumerate(weights):
        wait_sent(("weight", i), w.at[mine])
    wait_got("last", qf.at[:, 0:224])
    for plane in range(2):
        for part in range(2):
            four = [ff[part, plane, i].astype(F32) for i in range(4)]
            total = (four[0] + four[1]) + (four[2] + four[3])
            qs[0:32, :] = total
            for j in range(16):
                first_col = (plane * 32 + part * 16 + j) * HD
                out_ref[2:4, first_col:first_col + HD] = qs[pl.ds(j, 2, stride=16), :].astype(BF16)
    wait_sent("last", qf.at[:, 0:224])
    assert len(send_ids) <= N_SEND and len(recv_ids) <= N_RECV, (len(send_ids), len(recv_ids))


N_SEND = 10
N_RECV = 72


def local(
    queries, key_cache, value_cache, new_keys, new_values, lengths, resid_in, norm_gain,
    gate_weight, up_weight, down_weight,
):
    vmem = pl.BlockSpec(memory_space=pltpu.VMEM)
    smem = pl.BlockSpec(memory_space=pltpu.SMEM)
    hbm = pl.BlockSpec(memory_space=pl.ANY)
    both = pl.pallas_call(
        kernel,
        out_shape=jax.ShapeDtypeStruct((4, 8192), BF16),
        in_specs=[vmem, vmem, vmem, vmem, smem, vmem] + [hbm] * 5,
        out_specs=vmem,
        scratch_shapes=[
            pltpu.VMEM((2, CACHE, 1024), BF16),
            pltpu.VMEM((2, CACHE, 1024), BF16),
            pltpu.VMEM((2 * UNITS, PLANE), BF16),
            pltpu.VMEM((2 * UNITS, PLANE), BF16),
            pltpu.VMEM((2 * UNITS, PLANE), BF16),
            pltpu.VMEM((128, 128), F32),
            pltpu.VMEM((128, 128), F32),
            pltpu.VMEM((128, 128), F32),
            pltpu.VMEM((2, 2, 32, 128), BF16),
            pltpu.VMEM((2, 256, 128), BF16),
            pltpu.VMEM((256, 128), F32),
            pltpu.VMEM((2, 8, 4, 16, PART), BF16),
            pltpu.VMEM((2, 192, 2 * UNITS), F32),
            pltpu.VMEM((2, 512, 2 * UNITS), F32),
            pltpu.VMEM((2, 512, 2 * UNITS), F32),
            pltpu.VMEM((192, 2 * UNITS), F32),
            pltpu.VMEM((192, 2 * UNITS), BF16),
            pltpu.VMEM((192, 2 * UNITS), BF16),
            pltpu.VMEM((2, 8, 3, 16, PART), BF16),
            pltpu.VMEM((2, 8, 16, PART), F32),
            pltpu.VMEM((2, 2, 8, 16, HALF), BF16),
            pltpu.VMEM((2, 2, 8, 16, PART), BF16),
            pltpu.VMEM((2, 2, 4, 16, PART), BF16),
            pltpu.VMEM((2, 2, 4, 16, PART), BF16),
            pltpu.VMEM((2, 256, 128), BF16),
            pltpu.VMEM((2, 2, 4, 32, 128), BF16),
            pltpu.SemaphoreType.DMA((N_SEND,)),
            pltpu.SemaphoreType.DMA((N_RECV,)),
            pltpu.SemaphoreType.DMA((5,)),
        ],
        compiler_params=pltpu.CompilerParams(
            collective_id=0, has_side_effects=True, vmem_limit_bytes=56 * 2**20
        ),
        name="decode_layer",
    )(
        queries, resid_in, new_keys, new_values, lengths, norm_gain.reshape(64, 128),
        key_cache, value_cache, gate_weight, up_weight, down_weight,
    )
    return both[:2], both[2:]


def solution(mesh):
    rows = P(("side", "grp", "shard"), None)
    cache = P(("side", "grp", "shard"), None, None)
    return jax.shard_map(
        local,
        mesh=mesh,
        in_specs=(rows, cache, cache, rows, rows, P(("side", "grp", "shard")), rows, P(), rows, rows, rows),
        out_specs=(rows, rows),
        check_vma=False,
    )
```

```python
import jax
import jax.numpy as jnp
from jax import lax
from jax.experimental import pallas as pl
from jax.experimental.pallas import tpu as pltpu
from jax.sharding import PartitionSpec as P

MESH = pl.DeviceIdType.MESH
F32 = jnp.float32
BF16 = jnp.bfloat16

HD = 128
KVH = 8
CACHE = 192
UNITS = 208
EPSILON = 1e-05
NEG_FILL = -1e30

RING4 = (0, 1, -1, 2)
BACK4 = (0, 2, 1, 3)
GROUPS = ((0, 1), (1, 3), (3, 5), (5, 7), (7, 8))
DOTS = ((0, 1), (2,), (3, 4))
RUNS = ((0, 3), (3, 5), (5, 8))
BACKS = ((0, 3), (3, 5), (7, 8), (5, 7))
PLANE = 4096
PART = 2048
HALF = 1024
HALVES = (pl.ds(0, HALF), pl.ds(HALF, HALF))


def kernel(
    q_hbm, resid_hbm, newk_hbm, newv_hbm, len_ref, gain_hbm,
    k_hbm, v_hbm, gate_hbm, up_hbm, down_hbm,
    out_ref,
    q_ref, resid_ref, newk_ref, newv_ref, gain_ref, kb, vb, wg, wu, wd, qs, rs_, at, ns, r1, ex, xs, pa, pn, pr, haf, hab, hbb,
    tb, un, fr, cr, zs, zr, qf, ff,
    send_sems, recv_sems, local_sems,
):
    side = lax.axis_index("side")
    grp = lax.axis_index("grp")
    shard = lax.axis_index("shard")
    x = lax.rem(grp, 2) * 2 + side
    y = grp // 2
    z = shard // 2
    c = lax.rem(shard, 2)
    oc = 1 - c

    def device(dx=0, dy=0, dz=0, core=c):
        xx = lax.rem(x + dx + 4, 4)
        yy = lax.rem(y + dy + 4, 4)
        zz = lax.rem(z + dz + 8, 8)
        return (lax.rem(xx, 2), yy * 2 + xx // 2, zz * 2 + core)

    def along(part, d, core=c):
        return device(dx=d, core=core) if part == 0 else device(dy=d, core=core)

    def across(part, d, core=c):
        return along(1 - part, d, core)

    send_ids = {}
    recv_ids = {}

    def remote(src, dst, target, sent, got):
        i = send_ids.setdefault(sent, len(send_ids))
        j = recv_ids.setdefault(got, len(recv_ids))
        pltpu.make_async_remote_copy(
            src_ref=src, dst_ref=dst, send_sem=send_sems.at[i], recv_sem=recv_sems.at[j],
            device_id=target, device_id_type=MESH,
        ).start()

    def wait_sent(sent, ref):
        pltpu.make_async_copy(ref, ref, send_sems.at[send_ids[sent]]).wait()

    def wait_got(got, ref):
        pltpu.make_async_copy(ref, ref, recv_sems.at[recv_ids[got]]).wait()

    loads = []

    def local(src, dst):
        i = len(loads)
        loads.append(i)
        copy = pltpu.make_async_copy(src, dst, local_sems.at[i])
        copy.start()
        return copy

    row_loads = [local(h, w) for h, w in (
        (q_hbm, q_ref), (resid_hbm, resid_ref), (newk_hbm, newk_ref), (newv_hbm, newv_ref), (gain_hbm, gain_ref))]
    cache_loads = [local(k_hbm, kb), local(v_hbm, vb)]

    barrier = pltpu.get_barrier_semaphore()
    peers = [device(core=oc), device(dz=1), device(dz=-1)]
    for d in RING4[1:]:
        for core in (c, oc):
            peers.append(device(dx=d, core=core))
            peers.append(device(dy=d, core=core))
    for peer in peers:
        pl.semaphore_signal(barrier, inc=1, device_id=peer, device_id_type=MESH)

    mine = pl.ds(pl.multiple_of(c * UNITS, 16), UNITS)
    own_cols = pl.ds(pl.multiple_of(c * PLANE, PLANE), PLANE)
    other_cols = pl.ds(pl.multiple_of(oc * PLANE, PLANE), PLANE)
    weights = ((gate_hbm, wg), (up_hbm, wu), (down_hbm, wd))
    weight_loads = [local(h.at[:, own_cols], w.at[mine]) for h, w in weights]

    for load in row_loads:
        load.wait()
    qv = q_ref[...].astype(F32)
    rv = resid_ref[...].astype(F32)
    for j in range(64):
        qs[pl.ds(j, 2, stride=64), :] = qv[:, j * HD:(j + 1) * HD]
        rs_[pl.ds(j, 2, stride=64), :] = rv[:, j * HD:(j + 1) * HD]
    newk = newk_ref[...].astype(F32)
    newv = newv_ref[...].astype(F32)
    row = lax.broadcasted_iota(jnp.int32, (16, 2 * CACHE), 0)
    col = lax.broadcasted_iota(jnp.int32, (16, 2 * CACHE), 1)
    slot_of = jnp.where(row < 8, col, col - CACHE)
    filled = jnp.where(row < 8, len_ref[0], len_ref[1])
    valid = (slot_of >= 0) & (slot_of < filled)
    for load in cache_loads:
        load.wait()
    first = lax.broadcasted_iota(jnp.int32, (16, HD), 0) < 8

    def both(rows, k):
        one = rows[0:1, k * HD:(k + 1) * HD]
        two = rows[1:2, k * HD:(k + 1) * HD]
        return jnp.where(first, one, two)

    scale = HD ** (-0.5)
    scored = []
    for k in range(KVH):
        q16 = jnp.concatenate([qs[8 * k:8 * k + 8, :], qs[64 + 8 * k:72 + 8 * k, :]], axis=0)
        keys = kb[:, :, k * HD:(k + 1) * HD].reshape(2 * CACHE, HD)
        s = lax.dot_general(
            q16.astype(BF16), keys, (((1,), (1,)), ((), ())), preferred_element_type=F32
        ) * scale
        own = jnp.sum(q16 * both(newk, k), axis=1, keepdims=True) * scale
        scored.append((jnp.where(valid, s, NEG_FILL), own))
    weighted = []
    for s, own in scored:
        top = jnp.maximum(jnp.max(s, axis=1, keepdims=True), own)
        e = jnp.where(valid, jnp.exp(s - top), 0.0)
        own_e = jnp.exp(own - top)
        total = jnp.sum(e, axis=1, keepdims=True) + own_e
        weighted.append(((e / total).astype(BF16), (own_e / total).astype(BF16).astype(F32)))
    for k, (p, own_p) in enumerate(weighted):
        values = vb[:, :, k * HD:(k + 1) * HD].reshape(2 * CACHE, HD)
        mixed = jnp.dot(p, values, preferred_element_type=F32) + own_p * both(newv, k)
        for r in range(2):
            rows = pl.ds(r * 64 + 8 * k, 8)
            at[rows, :] = (rs_[rows, :] + mixed[8 * r:8 * r + 8]).astype(BF16).astype(F32)

    gain = gain_ref[...].astype(F32)
    for r in range(2):
        a = at[r * 64:(r + 1) * 64, :]
        mean_square = jnp.sum(a * a, keepdims=True).reshape(1, 1) * (1.0 / 8192)
        normed = (a * lax.rsqrt(mean_square + EPSILON) * gain).astype(BF16)
        for plane in range(2):
            for part in range(2):
                j = plane * 32 + part * 16
                ns[part, plane, r * 16:(r + 1) * 16, :] = normed[j:j + 16]

    pl.semaphore_wait(barrier, len(peers))

    def src_rows(slot, core):
        return pl.ds(pl.multiple_of((slot * 2 + core) * 32, 32), 32)

    for part in range(2):
        for d in (2, 1, -1):
            slot = BACK4[RING4.index(d)]
            for core in (c, oc):
                remote(ns.at[part, core], r1.at[part, src_rows(slot, c)], across(part, d, core), "first", ("first", part))
        remote(ns.at[part, oc], r1.at[part, src_rows(0, c)], device(core=oc), "first", ("first", part))
        r1[part, src_rows(0, c), :] = ns[part, c]
    for i, (h, w) in enumerate(weights):
        remote(h.at[:, other_cols], w.at[mine], device(core=oc), ("weight", i), ("weight", i))
    for j in range(64):
        out_ref[0:2, j * HD:(j + 1) * HD] = at[pl.ds(j, 2, stride=64), :].astype(BF16)

    def z_send(part, k, h):
        ahead, behind, hh = 2 * k, max(2 * k - 1, 0), HALVES[h]
        got = ("z", part, k, h)
        if k < 3 or h == 0:
            to = 2 * k + 2 if k < 3 else 7
            remote(xs.at[part, ahead, 0, :, hh], xs.at[part, to, 0, :, hh], device(dz=1), "z", got)
        if k < 3 or h == 1:
            remote(xs.at[part, behind, 0, :, hh], xs.at[part, 2 * k + 1, 0, :, hh], device(dz=-1), "z", got)

    def z_wait(part, k, h):
        hh = HALVES[h]
        wait_got(("z", part, k, h), xs.at[part, 2 * k + 1:2 * k + 3, 0, :, hh] if k < 3 else xs.at[part, 7, 0, :, hh])

    def x_send(part, g):
        zz = pl.ds(GROUPS[g][0], GROUPS[g][1] - GROUPS[g][0])
        remote(xs.at[part, zz, 0], xs.at[part, zz, 2], along(part, 1), "x", ("x", part, g))
        remote(xs.at[part, zz, 0], xs.at[part, zz, 1], along(part, -1), "x", ("x", part, g))

    def x_forward(part, g):
        zz = pl.ds(GROUPS[g][0], GROUPS[g][1] - GROUPS[g][0])
        wait_got(("x", part, g), xs.at[part, zz, 1:3])
        for s, h, d in ((2, HALVES[0], 1), (1, HALVES[1], -1)):
            remote(xs.at[part, zz, s, :, h], xs.at[part, zz, 3, :, h], along(part, d), "x", ("far", part, g))

    for part in range(2):
        wait_got(("first", part), r1.at[part, 0:224])
        ex[...] = r1[part].astype(F32)
        for j in range(16):
            xs[part, 0, 0, :, j * HD:(j + 1) * HD] = ex[pl.ds(j, 16, stride=16), :].astype(BF16)
        z_send(part, 0, 0)
        x_send(part, 0)
    for part in range(2):
        z_send(part, 0, 1)

    def gates(g, i):
        a, b = RUNS[g]
        n, m = b - a, 64 * (b - a)
        rows = pl.ds(a * 64, m)
        if i == 0:
            for part in range(2):
                for one in DOTS[g]:
                    wait_got(("far", part, one), xs.at[part, GROUPS[one][0]:GROUPS[one][1], 3])
        dots = [
            lax.dot_general(
                xs[part, a:b].reshape(m, PART), (wg, wu)[i][:, part * PART:(part + 1) * PART],
                (((1,), (1,)), ((), ())), preferred_element_type=F32,
            ) for part in range(2)
        ]
        for s in range(n):
            for u in range(4):
                for v in range(4):
                    pa[i, s * 64 + u * 16 + v * 4:s * 64 + u * 16 + v * 4 + 4, :] = (
                        dots[0][s * 64 + v * 16 + u * 4:s * 64 + v * 16 + u * 4 + 4])
        pn[i, rows, :] = pa[i, :m, :] + dots[1]
        remote(pn.at[i, rows], pr.at[i, rows], device(core=oc), "dots", ("dots", i, g))

    def hidden_down(g):
        a, b = RUNS[g]
        n, m = b - a, 64 * (b - a)
        rows = pl.ds(a * 64, m)
        wait_got(("dots", 0, g), pr.at[0, rows])
        gate = pn[0, rows, :] + pr[0, rows, :]
        wait_got(("dots", 1, g), pr.at[1, rows])
        up = pn[1, rows, :] + pr[1, rows, :]
        hidden = gate / (1.0 + jnp.exp(-gate)) * up
        hbb[:m, :] = hidden.astype(BF16)
        for s in range(n):
            for u in range(4):
                for v in range(4):
                    haf[s * 64 + u * 16 + v * 4:s * 64 + u * 16 + v * 4 + 4, :] = (
                        hidden[s * 64 + v * 16 + u * 4:s * 64 + v * 16 + u * 4 + 4])
        hab[:m, :] = haf[:m, :].astype(BF16)
        zz = pl.ds(a, n)
        for part, h in enumerate((hab, hbb)):
            for t in range(4):
                cols = pl.ds(t * 512, 512)
                term = jnp.dot(
                    h[:m, :], wd[:, part * PART + t * 512:part * PART + (t + 1) * 512],
                    preferred_element_type=F32,
                ).reshape(n, 4, 16, 512)
                un[part, zz, :, cols] = term[:, 0]
                tb[part, zz, :, :, cols] = term[:, 1:].astype(BF16)
            if g == 2:
                for one in (2, 3):
                    depart(part, one)
                for one in (2, 3):
                    depart_near(part, one)

    def depart(part, g):
        zz = pl.ds(BACKS[g][0], BACKS[g][1] - BACKS[g][0])
        for i, d in enumerate((1, -1)):
            remote(tb.at[part, zz, 2, :, HALVES[i]], fr.at[part, i, zz], along(part, d), "sum", ("relay", part, g))

    def depart_near(part, g):
        zz = pl.ds(BACKS[g][0], BACKS[g][1] - BACKS[g][0])
        for i, d in enumerate((1, -1)):
            h = HALVES[1 - i]
            remote(tb.at[part, zz, i, :, h], cr.at[part, i, zz, :, h], along(part, d), "sum", ("near", part, g))

    def depart_all(groups):
        for part in range(2):
            for g in groups:
                depart(part, g)
            for g in groups:
                depart_near(part, g)

    def relay(g):
        zz = pl.ds(BACKS[g][0], BACKS[g][1] - BACKS[g][0])
        for part in range(2):
            wait_got(("relay", part, g), fr.at[part, :, zz])
            for i, d in enumerate((1, -1)):
                h = HALVES[i]
                near = tb[part, zz, i, :, h].astype(F32) + fr[part, i, zz].astype(F32)
                tb[part, zz, i, :, h] = near.astype(BF16)
                remote(tb.at[part, zz, i, :, h], cr.at[part, i, zz, :, h], along(part, d), "sum", ("near", part, g))

    def collect(g):
        zz = pl.ds(BACKS[g][0], BACKS[g][1] - BACKS[g][0])
        for part in range(2):
            wait_got(("near", part, g), cr.at[part, :, zz])
            un[part, zz] = un[part, zz] + (cr[part, 0, zz].astype(F32) + cr[part, 1, zz].astype(F32))

    def z_step(k):
        for h in range(2):
            for part in range(2):
                z_wait(part, k - 1, h)
                if k < 4:
                    z_send(part, k, h)
                if h == 1:
                    x_send(part, k)

    def forward(g):
        for part in range(2):
            x_forward(part, g)

    def z_sum(step):
        for h in range(2):
            for part in range(2):
                hh = HALVES[h]
                if step > 0:
                    got = ("zsum", part, h, step - 1)
                    wait_got(got, zr.at[part, 0, 0, :, hh] if step == 1 else zr.at[part, :, step - 1, :, hh])
                if step == 4:
                    un[part, 0, :, hh] = un[part, 0, :, hh] + (
                        zr[part, 0, 3, :, hh].astype(F32) + zr[part, 1, 3, :, hh].astype(F32))
                    continue
                for i, d in enumerate((1, -1)):
                    if step == 0 and i != h:
                        continue
                    total = un[part, 7 if step == 0 else 2 * (4 - step) - 1 + i, :, hh]
                    if step > 1 or (step == 1 and i == h):
                        total = total + zr[part, i, step - 1, :, hh].astype(F32)
                    zs[part, i, step, :, hh] = total.astype(BF16)
                    remote(zs.at[part, i, step, :, hh], zr.at[part, i, step, :, hh], device(dz=d),
                           "zsum", ("zsum", part, h, step))

    z_step(1)
    forward(0)
    z_step(2)
    forward(1)
    z_step(3)
    forward(2)
    for copy in weight_loads:
        copy.wait()
    for i, (h, w) in enumerate(weights):
        wait_got(("weight", i), w.at[mine])
    gates(0, 0)
    z_step(4)
    gates(0, 1)
    forward(3)
    hidden_down(0)
    forward(4)
    depart_all((0,))
    gates(1, 0)
    gates(1, 1)
    gates(2, 0)
    gates(2, 1)
    hidden_down(1)
    relay(0)
    hidden_down(2)
    relay(2)
    relay(3)
    depart_all((1,))
    collect(0)
    collect(2)
    z_sum(0)
    relay(1)
    collect(3)
    z_sum(1)
    collect(1)
    z_sum(2)
    z_sum(3)
    z_sum(4)

    for part in range(2):
        for j in range(16):
            ex[pl.ds(j, 16, stride=16), :] = un[part, 0, :, j * HD:(j + 1) * HD]
        qf[part] = ex[...].astype(BF16)
        for s, d in ((3, 2), (1, 1), (2, -1)):
            for core in (c, oc):
                remote(qf.at[part, src_rows(s, core)], ff.at[part, c, BACK4[s]], across(part, d, core), "last", "last")
        remote(qf.at[part, src_rows(0, oc)], ff.at[part, c, 0], device(core=oc), "last", "last")
        ff[part, c, 0] = qf[part, src_rows(0, c), :]
    for sent, ref in (
        ("first", r1.at[:, 0:224]), ("z", xs.at[:, 0:7, 0]), ("x", xs.at[:, :, 0:3]), ("dots", pn),
        ("sum", tb), ("zsum", xs.at[:, 0:7, 0]),
    ):
        wait_sent(sent, ref)
    for i, (h, w) in enumerate(weights):
        wait_sent(("weight", i), w.at[mine])
    wait_got("last", qf.at[:, 0:224])
    for plane in range(2):
        for part in range(2):
            four = [ff[part, plane, i].astype(F32) for i in range(4)]
            total = (four[0] + four[1]) + (four[2] + four[3])
            qs[0:32, :] = total
            for j in range(16):
                first_col = (plane * 32 + part * 16 + j) * HD
                out_ref[2:4, first_col:first_col + HD] = qs[pl.ds(j, 2, stride=16), :].astype(BF16)
    wait_sent("last", qf.at[:, 0:224])
    assert len(send_ids) <= N_SEND and len(recv_ids) <= N_RECV, (len(send_ids), len(recv_ids))


N_SEND = 10
N_RECV = 80


def local(
    queries, key_cache, value_cache, new_keys, new_values, lengths, resid_in, norm_gain,
    gate_weight, up_weight, down_weight,
):
    vmem = pl.BlockSpec(memory_space=pltpu.VMEM)
    smem = pl.BlockSpec(memory_space=pltpu.SMEM)
    hbm = pl.BlockSpec(memory_space=pl.ANY)
    both = pl.pallas_call(
        kernel,
        out_shape=jax.ShapeDtypeStruct((4, 8192), BF16),
        in_specs=[hbm, hbm, hbm, hbm, smem, hbm] + [hbm] * 5,
        out_specs=vmem,
        scratch_shapes=[
            pltpu.VMEM((2, 8192), BF16),
            pltpu.VMEM((2, 8192), BF16),
            pltpu.VMEM((2, 1024), BF16),
            pltpu.VMEM((2, 1024), BF16),
            pltpu.VMEM((64, 128), BF16),
            pltpu.VMEM((2, CACHE, 1024), BF16),
            pltpu.VMEM((2, CACHE, 1024), BF16),
            pltpu.VMEM((2 * UNITS, PLANE), BF16),
            pltpu.VMEM((2 * UNITS, PLANE), BF16),
            pltpu.VMEM((2 * UNITS, PLANE), BF16),
            pltpu.VMEM((128, 128), F32),
            pltpu.VMEM((128, 128), F32),
            pltpu.VMEM((128, 128), F32),
            pltpu.VMEM((2, 2, 32, 128), BF16),
            pltpu.VMEM((2, 256, 128), BF16),
            pltpu.VMEM((256, 128), F32),
            pltpu.VMEM((2, 8, 4, 16, PART), BF16),
            pltpu.VMEM((2, 192, 2 * UNITS), F32),
            pltpu.VMEM((2, 512, 2 * UNITS), F32),
            pltpu.VMEM((2, 512, 2 * UNITS), F32),
            pltpu.VMEM((192, 2 * UNITS), F32),
            pltpu.VMEM((192, 2 * UNITS), BF16),
            pltpu.VMEM((192, 2 * UNITS), BF16),
            pltpu.VMEM((2, 8, 3, 16, PART), BF16),
            pltpu.VMEM((2, 8, 16, PART), F32),
            pltpu.VMEM((2, 2, 8, 16, HALF), BF16),
            pltpu.VMEM((2, 2, 8, 16, PART), BF16),
            pltpu.VMEM((2, 2, 4, 16, PART), BF16),
            pltpu.VMEM((2, 2, 4, 16, PART), BF16),
            pltpu.VMEM((2, 256, 128), BF16),
            pltpu.VMEM((2, 2, 4, 32, 128), BF16),
            pltpu.SemaphoreType.DMA((N_SEND,)),
            pltpu.SemaphoreType.DMA((N_RECV,)),
            pltpu.SemaphoreType.DMA((10,)),
        ],
        compiler_params=pltpu.CompilerParams(
            collective_id=0, has_side_effects=True, vmem_limit_bytes=56 * 2**20
        ),
        name="decode_layer",
    )(
        queries, resid_in, new_keys, new_values, lengths, norm_gain.reshape(64, 128),
        key_cache, value_cache, gate_weight, up_weight, down_weight,
    )
    return both[:2], both[2:]


def solution(mesh):
    rows = P(("side", "grp", "shard"), None)
    cache = P(("side", "grp", "shard"), None, None)
    return jax.shard_map(
        local,
        mesh=mesh,
        in_specs=(rows, cache, cache, rows, rows, P(("side", "grp", "shard")), rows, P(), rows, rows, rows),
        out_specs=(rows, rows),
        check_vma=False,
    )
```
